1024 devices in a mesh: dp: 16 (over y_hi, x), expert: 32 (over z, core), pair: 2 (over y_lo).
Axes of the slice: x: 4, y: 8 (y_hi: 4, y_lo: 2; y = y_hi * 2 + y_lo), z: 16, core: 2. Of those that a mesh axis runs over, the one named last changes fastest.
Arguments:
- tokens: bfloat16 [1024, 7168], P('expert', 'pair'), may hold values from -6 to 6
- routes: int32 [1024, 8], P('expert'), may hold values from 0 to 31, all different within a row; in each aligned block of 32 rows (0 to 31, 32 to 63, ...) at most 16 rows name the same one
- gates: float32 [1024, 8], P('expert'), may hold values from 0.05 to 0.6
- w_gate: bfloat16 [32, 7168, 2048], P('expert', 'pair', 'dp'), may hold values from -0.0625 to 0.0625
- w_up: bfloat16 [32, 7168, 2048], P('expert', 'pair', 'dp'), may hold values from -0.0625 to 0.0625
- w_down: bfloat16 [32, 2048, 7168], P('expert', 'dp', 'pair'), may hold values from -0.125 to 0.125
Outputs:
- mixed: bfloat16 [1024, 7168], P('expert', 'pair')
The draws below stay inside these ranges and needn't reach their ends.
Inputs may be any that keep to these rules, and one draw needn't show every extreme that they name: `routes`: each row names 8 different experts. Among the rows of one device's block of 32 tokens no expert is named more than 16 times, and in every draw some expert is named exactly 16 times in some block.
All inputs are finite; a program needn't handle non-finite values.
Results may differ from the reference program's by a relative error of at most 0.03.
Values may be sent and summed in bfloat16 or wider, within the bound.
A program may use at most 32 MiB of HBM per device.

```python
import math
import jax
import jax.numpy as jnp
import numpy as np
from jax import lax

D = 7168
FF = 2048
TOPK = 8
EXPERTS = 32
TOK_DEV = 32
CAP = 16
TOKENS = 1024
N_DP = 16
N_EXPERT = 32


def levels(stream_key, extent, cuts, smallest, largest):
    gain = 1.0
    for position, parts in cuts:
        draws = jax.random.uniform(jax.random.fold_in(jax.random.fold_in(stream_key, 6), position), (parts,), jnp.float32, smallest / len(cuts), largest / len(cuts))
        gain = gain * jnp.repeat(jnp.exp(draws), extent[position] // parts).reshape((-1,) + (1,) * (len(extent) - 1 - position))
    return gain


def assign_block(stream_key, own, number, rows, amount, top, reach, slope):
    order = jax.random.permutation(stream_key, amount)
    heavy_load, usual = load_shares(amount, rows * top, reach, slope, True), load_shares(amount, rows * top, reach, slope, False)
    places = jnp.arange(amount)

    def named(lengths, turn):
        used = int((lengths > 0).sum())
        fixed = max(1, used // 4)
        shifted = fixed + (places - fixed + turn * (used - fixed)) % max(1, amount - fixed)
        return jnp.zeros((amount,), jnp.int32).at[order[jnp.where(places < fixed, places, shifted)]].set(jnp.asarray(lengths, jnp.int32))

    lengths = jnp.where(number % 4 == 0, named(heavy_load, number // 4), named(usual, number - number // 4 - 1))
    mixed = jax.random.permutation(jax.random.fold_in(own, 3), amount)
    giver, receiver = mixed[0:amount // 2 * 2:2], mixed[1:amount // 2 * 2:2]
    room = jnp.minimum(lengths[giver] - 1, reach - lengths[receiver]) // 2
    room = jnp.where((giver == order[0]) | (receiver == order[0]) | (lengths[receiver] == 0), 0, jnp.maximum(room, 0))
    shifted = jax.random.randint(jax.random.fold_in(own, 4), (amount // 2,), 0, 1 << 20) % (room + 1)
    lengths = lengths.at[giver].add(-shifted).at[receiver].add(shifted)
    items = jnp.searchsorted(jnp.cumsum(lengths), jnp.arange(rows * top), side="right").astype(jnp.int32)
    table = items.reshape(top, rows).T
    table = table[jax.random.permutation(jax.random.fold_in(own, 1), rows)]
    turn = jax.random.randint(jax.random.fold_in(own, 2), (rows, 1), 0, top)
    return jnp.take_along_axis(table, (jnp.arange(top)[None, :] + turn) % top, axis=1)


def load_shares(amount, total, reach, slope, full):
    loads = [(1 << 20) // math.isqrt(rank ** slope) + 1 for rank in range(1, amount + 1)]
    largest = reach if full else min(reach, max(-(-total // amount), total * loads[0] // sum(loads)))
    least = 1 if total - largest >= amount - 1 else 0
    holding, rest = [largest] + [least] * (amount - 1), total - largest - least * (amount - 1)
    while rest > 0:
        free = [i for i in range(1, amount) if holding[i] < largest] or [i for i in range(1, amount) if holding[i] < reach]
        mass, remaining = sum([loads[i] for i in free]), rest
        for i in free:
            addition = min(reach - holding[i], max(1, remaining * loads[i] // mass), rest)
            holding[i] = holding[i] + addition
            rest = rest - addition
    return np.array(holding)


def normal_values(own_key, dims, width, most, split=(), kind=jnp.bfloat16):
    drawn = jax.random.normal(own_key, dims, jnp.float32) * width
    if len(split) > 0:
        drawn = levels(own_key, dims, split, -0.22, 0.18) * drawn
    return jnp.clip(drawn, min=-most, max=most).astype(kind)


def setup_inputs(seed: int = 0) -> dict:
    streams_of = jax.random.split(jax.random.key(seed), 7)
    tokens = normal_values(streams_of[0], (TOKENS, D), 1.0, 6.0, ((0, 32), (1, 2)))
    routes_keys = jax.random.split(jax.random.fold_in(streams_of[1], 1), TOKENS // TOK_DEV)
    routes_turns = jax.random.permutation(jax.random.fold_in(streams_of[1], 3), TOKENS // TOK_DEV)
    routes = jax.vmap(lambda own, number: assign_block(jax.random.fold_in(streams_of[1], 2), own, number, TOK_DEV, EXPERTS, TOPK, CAP, 2))(routes_keys, routes_turns).reshape((TOKENS, TOPK))
    gates = jnp.clip(0.05 + 0.55 * jax.random.uniform(streams_of[2], (TOKENS, TOPK), jnp.float32) ** levels(streams_of[2], (TOKENS, TOPK), ((0, 32),), -0.2, 0.2), 0.05, 0.6)
    w_gate = normal_values(streams_of[3], (EXPERTS, D, FF), D ** -0.5, 0.0625, ((0, 32), (1, 2), (2, 16)))
    w_up = normal_values(streams_of[4], (EXPERTS, D, FF), D ** -0.5, 0.0625, ((0, 32), (1, 2), (2, 16)))
    w_down = normal_values(streams_of[5], (EXPERTS, FF, D), FF ** -0.5, 0.125, ((0, 32), (1, 16), (2, 2)))
    return dict(tokens=tokens, routes=routes, gates=gates, w_gate=w_gate, w_up=w_up, w_down=w_down)


def route_slots(routes):
    blocks = routes.reshape(N_EXPERT, TOK_DEV * TOPK)
    onehot = (blocks[:, :, None] == jnp.arange(EXPERTS, dtype=jnp.int32)[None, None, :]).astype(jnp.int32)
    before = jnp.cumsum(onehot, axis=1) - onehot
    return blocks, jnp.sum(before * onehot, axis=2).astype(jnp.int32)


def reference(tokens, routes, gates, w_gate, w_up, w_down):
    blocks, slot_index = route_slots(routes)
    block_ids = jnp.broadcast_to(jnp.arange(N_EXPERT, dtype=jnp.int32)[:, None], blocks.shape)
    token_ids = block_ids * TOK_DEV + (jnp.arange(TOK_DEV * TOPK, dtype=jnp.int32) // TOPK)[None, :]
    positions = (block_ids * CAP + slot_index).astype(jnp.int32)
    slot_table = jnp.full((EXPERTS, N_EXPERT * CAP), TOKENS, jnp.int32)
    slot_table = slot_table.at[blocks, positions].set(token_ids.astype(jnp.int32))
    padded = jnp.concatenate([tokens, jnp.zeros((1, D), tokens.dtype)], axis=0)

    def one_expert(operands):
        row_index, gate_matrix, up_matrix, down_matrix = operands
        dispatched = padded[row_index]
        gate_sum = jnp.dot(dispatched, gate_matrix, preferred_element_type=jnp.float32)
        up_sum = jnp.dot(dispatched, up_matrix, preferred_element_type=jnp.float32)
        hidden = (jax.nn.silu(gate_sum) * up_sum).astype(jnp.bfloat16)
        grouped = hidden.reshape(N_EXPERT * CAP, N_DP, FF // N_DP).astype(jnp.float32)
        down_groups = down_matrix.reshape(N_DP, FF // N_DP, D).astype(jnp.float32)
        group_parts = jnp.einsum('rgf,gfd->grd', grouped, down_groups).astype(jnp.bfloat16)
        group_parts = lax.optimization_barrier(group_parts)
        return jnp.sum(group_parts.astype(jnp.float32), axis=0).astype(jnp.bfloat16)

    expert_out = lax.map(one_expert, (slot_table, w_gate, w_up, w_down))
    picked = expert_out[blocks, positions].reshape(TOKENS, TOPK, D).astype(jnp.float32)
    mixed = jnp.sum(gates[:, :, None] * picked, axis=1)
    return mixed.astype(jnp.bfloat16)
```

```python
import jax
import jax.numpy as jnp
from jax import lax
from jax.experimental import pallas as pl
from jax.experimental.pallas import tpu as pltpu
from jax.sharding import PartitionSpec as P

MESH = pl.DeviceIdType.MESH
NX = 4
NY = 4
NZ = 16
NCORE = 2
BLOCK = 32
HALF = 3584
QUART = 896
SUB = 256
FFS = 128
CHUNKS = 8
PER = 2
CUT = 32
NB = 2
ROWS = PER * BLOCK
OFFSETS = (1, -1, 2, -2, 3, -3, 4, -4, 5, -5, 6, -6, 7, -7, 8, 0)
OWN = NZ - 1
JUMP = 2
TOPK = 8
ORDER = (('A', (0,)), ('A', (1,)), ('F', (0,)), ('A', (2,)), ('F', (1,)), ('A', (3,)), ('B', (0,)), ('F', (2,)), ('A', (4,)), ('B', (1,)), ('A', (5,)), ('F', (3,)), ('C', (0,)), ('B', (2,)), ('A', (6,)), ('F', (4,)), ('C', (1,)), ('A', (7,)), ('F', (5,)), ('B', (3,)), ('G', (0,)), ('C', (2,)), ('F', (6,)), ('B', (4,)), ('C', (3,)), ('G', (1,)), ('F', (7,)), ('B', (5,)), ('D', (0,)), ('C', (4,)), ('G', (2,)), ('B', (6,)), ('C', (5,)), ('G', (3,)), ('D', (1,)), ('E', (0,)), ('B', (7,)), ('C', (6,)), ('G', (4,)), ('D', (2,)), ('E', (1,)), ('G', (5,)), ('C', (7,)), ('D', (3,)), ('G', (6,)), ('E', (2,)), ('D', (4,)), ('D', (5,)), ('G', (7,)), ('E', (3,)), ('D', (6,)), ('E', (4,)), ('D', (7,)), ('E', (5,)), ('E', (6,)), ('E', (7,)))


def kernel(
    tok, routes, gates, wg, wu, wd, out,
    x_all, w_gu, w_d, meta, gu_own, gu_send, gu_recv, part, xr, ys, yr, zs, zr, fo,
    w_loc, w_send, w_recv, zg_send, zg_recv, mg_send, mg_recv, bg_send, bg_recv, xg_send, xg_recv,
    xf_send, xf_recv, yg_send, yg_recv,
    p_send, p_recv, xr_send, xr_recv, xc_send, xc_recv, yr_send, yr_recv, zr_send, zr_recv, ag_send, ag_recv,
):
    dp = lax.axis_index("dp")
    ex = lax.axis_index("expert")
    pr = lax.axis_index("pair")
    yh, x = dp // NX, lax.rem(dp, NX)
    z, core = ex // NCORE, lax.rem(ex, NCORE)

    def at_z(off):
        return {"expert": lax.rem(z + (off + NZ), NZ) * NCORE + core}

    def at_x(d):
        return {"dp": yh * NX + lax.rem(x + d, NX)}

    x1, x2, x3 = (lax.rem(x + d, NX) for d in (1, 2, 3))

    def at_y(d):
        return {"dp": lax.rem(yh + d, NY) * NX + x}

    def at_dp(d):
        return {"dp": lax.rem(dp + d, NX * NY)}

    sibling = {"expert": z * NCORE + (1 - core)}
    partner = {"pair": 1 - pr}

    def remote(src, dst, send, recv, where):
        return pltpu.make_async_remote_copy(
            src_ref=src, dst_ref=dst, send_sem=send, recv_sem=recv,
            device_id=where, device_id_type=MESH,
        )

    barrier = pltpu.get_barrier_semaphore()
    for k in range(NZ - 1):
        pl.semaphore_signal(barrier, inc=1, device_id=at_z(OFFSETS[k]), device_id_type=MESH)
    for d in range(1, NX * NY):
        pl.semaphore_signal(barrier, inc=1, device_id=at_dp(d), device_id_type=MESH)
    pl.semaphore_signal(barrier, inc=1, device_id=sibling, device_id_type=MESH)
    pl.semaphore_signal(barrier, inc=1, device_id=partner, device_id_type=MESH)

    wcol = pl.multiple_of(core * FFS, FFS)
    wcol_up = pl.multiple_of((NCORE + core) * FFS, FFS)
    w_dsts = (
        (wg.at[0], w_gu.at[:, pl.ds(wcol, FFS)]),
        (wu.at[0], w_gu.at[:, pl.ds(wcol_up, FFS)]),
        (wd.at[0], w_d.at[pl.ds(wcol, FFS)]),
    )
    local = [pltpu.make_async_copy(s, d, w_loc.at[i]) for i, (s, d) in enumerate(w_dsts)]
    own = slice(OWN * BLOCK, NZ * BLOCK)
    mine_in = pltpu.make_async_copy(tok, x_all.at[own], w_loc.at[3])
    mine_in.start()
    for cp in local:
        cp.start()

    lane = lax.broadcasted_iota(jnp.int32, (BLOCK, 128), 1)
    first = jnp.zeros((BLOCK, 128), jnp.float32)
    second = jnp.zeros((BLOCK, 128), jnp.float32)
    for k in range(TOPK):
        r = routes[:, k : k + 1]
        g = gates[:, k : k + 1]
        first = first + jnp.where(lane == r, g, 0.0)
        second = second + jnp.where(lane == r + 32, g, 0.0)
    low = second - second.astype(jnp.bfloat16).astype(jnp.float32)
    meta[own, :] = jnp.where(lane < 32, first, low).astype(jnp.bfloat16)
    ys[:, QUART:] = jnp.zeros((CHUNKS * ROWS, NY * SUB - QUART), jnp.bfloat16)

    mine_in.wait()
    pl.semaphore_wait(barrier, NZ - 1 + NX * NY - 1 + 2)

    nb = NB * 128
    na = QUART - nb
    qcol = pl.multiple_of(x * QUART, 128)
    acol = pl.ds(pl.multiple_of(x * na, 128), na)
    bcol = pl.ds(pl.multiple_of(NX * na + yh * nb, 128), nb) if nb else None
    pieces = [(meta, slice(None), mg_send, mg_recv), (x_all, acol, zg_send, zg_recv)]
    if nb:
        pieces.append((x_all, bcol, bg_send, bg_recv))
    sends = []
    zgot = {}

    def hop(src, k):
        step = OFFSETS[k] if src == OWN else (JUMP if OFFSETS[k] > 0 else -JUMP)
        cps = []
        for ref, cols, ssem, rsem in pieces:
            cp = remote(
                ref.at[pl.ds(src * BLOCK, BLOCK), cols], ref.at[pl.ds(k * BLOCK, BLOCK), cols],
                ssem.at[k], rsem.at[k], at_z(step),
            )
            cp.start()
            cps.append(cp)
        zgot[k] = cps
        sends.extend(cps)

    for k in range(2 * JUMP):
        hop(OWN, k)
    weights = [
        remote(s, d, w_send.at[i], w_recv.at[i], sibling) for i, (s, d) in enumerate(w_dsts)
    ]
    for cp in weights:
        cp.start()
    sends += weights

    gathered = {}
    halves = {}
    paired = {}
    xred = {}
    xcom = {}
    yred = {}
    zred = {}

    def stage_a(j):
        for k in range(PER * j, PER * j + PER):
            if k == OWN:
                continue
            for cp in zgot[k]:
                cp.wait_recv()
            if k + 2 * JUMP < OWN:
                hop(k, k + 2 * JUMP)
        count = ROWS - BLOCK if j == CHUNKS - 1 else ROWS
        rows = pl.ds(ROWS * j, count)
        where = x_all.at[rows, acol]
        cps = [
            remote(where, where, xg_send.at[j, d - 1], xg_recv.at[j, d - 1], at_x(d))
            for d in (1, 3)
        ]
        halves[j] = cps
        ycps = []
        if nb:
            where = x_all.at[rows, bcol]
            ycps = [
                remote(where, where, yg_send.at[j, d - 1], yg_recv.at[j, d - 1], at_y(d))
                for d in (2, 1, 3)
            ]
        for cp in cps + ycps:
            cp.start()
        gathered[j] = list(ycps)
        sends.extend(cps + ycps)

    def stage_f(j):
        count = ROWS - BLOCK if j == CHUNKS - 1 else ROWS
        cut = count // 2
        for i, (cp, d) in enumerate(zip(halves[j], (1, 3))):
            cp.wait_recv()
            low, size = (0, cut) if i == 0 else (cut, count - cut)
            came = pl.ds(pl.multiple_of(lax.rem(x + (NX - d), NX) * na, 128), na)
            where = x_all.at[pl.ds(ROWS * j + low, size), came]
            f = remote(where, where, xf_send.at[j, i], xf_recv.at[j, i], at_x(d))
            f.start()
            gathered[j].append(f)
            sends.append(f)

    def stage_b(j):
        if j == 0:
            for cp in local:
                cp.wait()
            for cp in weights:
                cp.wait_recv()
        for cp in gathered[j]:
            cp.wait_recv()
        rows = pl.ds(j * ROWS, ROWS)

        def column(n, carry):
            cols = pl.ds(pl.multiple_of(n * 256, 256), 256)
            v = jnp.dot(x_all[rows, :], w_gu[:, cols], preferred_element_type=jnp.float32)
            gu_own[rows, cols] = v
            gu_send[rows, cols] = v.astype(jnp.bfloat16)
            return carry

        lax.fori_loop(0, 2, column, 0)
        cp = remote(gu_send.at[rows], gu_recv.at[rows], p_send.at[j], p_recv.at[j], partner)
        cp.start()
        paired[j] = cp
        sends.append(cp)

    def stage_c(j):
        paired[j].wait_recv()
        rows = pl.ds(j * ROWS, ROWS)
        m = meta[rows, :].astype(jnp.float32)
        lanes = lax.broadcasted_iota(jnp.int32, (ROWS, 128), 1)
        hidden = []
        for c in range(NCORE):
            e = z * NCORE + c
            mine = (lanes == e) | (lanes == e + 32)
            weight = jnp.sum(jnp.where(mine, m, 0.0), axis=1, keepdims=True)
            gcols = slice(c * FFS, (c + 1) * FFS)
            ucols = slice((NCORE + c) * FFS, (NCORE + c + 1) * FFS)
            g = gu_own[rows, gcols] + gu_recv[rows, gcols].astype(jnp.float32)
            u = gu_own[rows, ucols] + gu_recv[rows, ucols].astype(jnp.float32)
            h = (0.5 * g) * (1.0 + jnp.tanh(0.5 * g)) * u * weight
            hidden.append(h.astype(jnp.bfloat16))
        hidden = jnp.concatenate(hidden, axis=1)
        def quarter(q, carry):
            v = jnp.dot(
                hidden, w_d[:, pl.ds(pl.multiple_of(q * QUART, 128), QUART)],
                preferred_element_type=jnp.float32,
            )
            part[q, rows, :] = v.astype(jnp.bfloat16)
            return carry

        lax.fori_loop(0, NX, quarter, 0)
        low, high = pl.ds(j * ROWS, CUT), pl.ds(j * ROWS + CUT, ROWS - CUT)
        cps = []
        for i, (d, q, half, slot) in enumerate(
            ((1, x2, low, 2), (3, x2, high, 3), (1, x1, high, 0), (3, x3, low, 1))
        ):
            cp = remote(
                part.at[q, half], xr.at[slot, half], xr_send.at[j, i], xr_recv.at[j, i], at_x(d)
            )
            cp.start()
            cps.append(cp)
        xred[j] = cps
        sends.extend(cps)

    def stage_g(j):
        low, high = pl.ds(j * ROWS, CUT), pl.ds(j * ROWS + CUT, ROWS - CUT)
        cps = []
        for i, (d, q, half) in enumerate(((1, x1, low), (3, x3, high))):
            xred[j][i].wait_recv()
            v = part[q, half, :].astype(jnp.float32) + xr[2 + i, half, :].astype(jnp.float32)
            part[q, half, :] = v.astype(jnp.bfloat16)
            cp = remote(
                part.at[q, half], xr.at[i, half], xc_send.at[j, i], xc_recv.at[j, i], at_x(d)
            )
            cp.start()
            cps.append(cp)
        xcom[j] = cps
        sends.extend(cps)

    def stage_d(j):
        for cp in xred[j][2:] + xcom[j]:
            cp.wait_recv()
        rows = pl.ds(j * ROWS, ROWS)
        total = part[x, rows, :].astype(jnp.float32)
        for d in range(2):
            total = total + xr[d, rows, :].astype(jnp.float32)
        ys[rows, 0:QUART] = total.astype(jnp.bfloat16)
        cps = []
        for d in (2, 1, 3):
            scol = pl.multiple_of(lax.rem(yh + d, NY) * SUB, SUB)
            cp = remote(
                ys.at[rows, pl.ds(scol, SUB)], yr.at[d - 1, rows],
                yr_send.at[j, d - 1], yr_recv.at[j, d - 1], at_y(d),
            )
            cp.start()
            cps.append(cp)
        yred[j] = cps
        sends.extend(cps)

    def stage_e(j):
        for cp in yred[j]:
            cp.wait_recv()
        rows = pl.ds(j * ROWS, ROWS)
        total = ys[rows, pl.ds(pl.multiple_of(yh * SUB, SUB), SUB)].astype(jnp.float32)
        for d in range(NY - 1):
            total = total + yr[d, rows, :].astype(jnp.float32)
        zs[rows, :] = total.astype(jnp.bfloat16)
        for k in range(PER * j, PER * j + PER):
            if k != OWN:
                cp = remote(
                    zs.at[pl.ds(k * BLOCK, BLOCK)], zr.at[k],
                    zr_send.at[k], zr_recv.at[k], at_z(-OFFSETS[k]),
                )
                cp.start()
                zred[k] = cp
                sends.append(cp)

    stages = dict(A=stage_a, F=stage_f, G=stage_g, B=stage_b, C=stage_c, D=stage_d, E=stage_e)
    for name, numbers in ORDER :
        for j in numbers:
            stages[name](j)

    total = zs[own, :].astype(jnp.float32)
    for k in range(NZ - 1):
        zred[k].wait_recv()
        total = total + zr[k].astype(jnp.float32)
    fo[dp] = total.astype(jnp.bfloat16)
    last = []
    for d in range(1, NX * NY):
        cp = remote(fo.at[dp], fo.at[dp], ag_send.at[d], ag_recv.at[d], at_dp(d))
        cp.start()
        last.append(cp)
    sends += last
    for cp in last:
        cp.wait_recv()
    for b in range(NY):
        for a in range(NX):
            width = min(SUB, QUART - b * SUB)
            start = a * QUART + b * SUB
            out[:, start : start + width] = fo[b * NX + a, :, 0:width]
    for cp in sends:
        cp.wait_send()


def per_device(tokens, routes, gates, w_gate, w_up, w_down):
    total = CHUNKS * ROWS
    bf, f32 = jnp.bfloat16, jnp.float32
    dma = pltpu.SemaphoreType.DMA
    vm = pl.BlockSpec(memory_space=pltpu.VMEM)
    hbm = pl.BlockSpec(memory_space=pl.ANY)
    return pl.pallas_call(
        kernel,
        out_shape=jax.ShapeDtypeStruct((BLOCK, HALF), bf),
        in_specs=[hbm, vm, vm, hbm, hbm, hbm],
        out_specs=vm,
        scratch_shapes=[
            pltpu.VMEM((total, HALF), bf),
            pltpu.VMEM((HALF, 2 * NCORE * FFS), bf),
            pltpu.VMEM((NCORE * FFS, HALF), bf),
            pltpu.VMEM((total, 128), bf),
            pltpu.VMEM((total, 2 * NCORE * FFS), f32),
            pltpu.VMEM((total, 2 * NCORE * FFS), bf),
            pltpu.VMEM((total, 2 * NCORE * FFS), bf),
            pltpu.VMEM((NX, total, QUART), bf),
            pltpu.VMEM((NX, total, QUART), bf),
            pltpu.VMEM((total, NY * SUB), bf),
            pltpu.VMEM((NY - 1, total, SUB), bf),
            pltpu.VMEM((total, SUB), bf),
            pltpu.VMEM((NZ, BLOCK, SUB), bf),
            pltpu.VMEM((NX * NY, BLOCK, SUB), bf),
            dma((4,)), dma((3,)), dma((3,)),
            dma((NZ,)), dma((NZ,)), dma((NZ,)), dma((NZ,)),
            dma((NZ,)), dma((NZ,)),
            dma((CHUNKS, NX - 1)), dma((CHUNKS, NX - 1)),
            dma((CHUNKS, 2)), dma((CHUNKS, 2)),
            dma((CHUNKS, NY - 1)), dma((CHUNKS, NY - 1)),
            dma((CHUNKS,)), dma((CHUNKS,)),
            dma((CHUNKS, 4)), dma((CHUNKS, 4)),
            dma((CHUNKS, 2)), dma((CHUNKS, 2)),
            dma((CHUNKS, NY - 1)), dma((CHUNKS, NY - 1)),
            dma((NZ,)), dma((NZ,)),
            dma((NX * NY,)), dma((NX * NY,)),
        ],
        compiler_params=pltpu.CompilerParams(
            collective_id=0, has_side_effects=True, vmem_limit_bytes=60 << 20
        ),
        cost_estimate=pl.CostEstimate(flops=2 * 3 * 512 * 3584 * 256, bytes_accessed=4 << 20, transcendentals=512 * 256),
    )(tokens, routes, gates, w_gate, w_up, w_down)


def solution(mesh):
    placed = (
        P("expert", "pair"),
        P("expert", None),
        P("expert", None),
        P("expert", "pair", "dp"),
        P("expert", "pair", "dp"),
        P("expert", "dp", "pair"),
    )
    return jax.shard_map(
        per_device, mesh=mesh, in_specs=placed, out_specs=P("expert", "pair"), check_vma=False
    )
```

```python
import jax
import jax.numpy as jnp
from jax import lax
from jax.experimental import pallas as pl
from jax.experimental.pallas import tpu as pltpu
from jax.sharding import PartitionSpec as P

MESH = pl.DeviceIdType.MESH
NX = 4
NY = 4
NZ = 16
NCORE = 2
BLOCK = 32
HALF = 3584
QUART = 896
SUB = 256
FFS = 128
STARTS = (0, 2, 4, 6, 8, 10, 12, 14, 15, 16)
CHUNKS = 9
ALONE = CHUNKS - 1
NB = 2
TOTAL = 512
OFFSETS = (1, -1, 2, -2, 3, -3, 4, -4, 5, -5, 6, -6, 7, -7, 8, 0)
OWN = NZ - 1
JUMP = 2
TOPK = 8
ORDER = (
    ("A", 0), ("A", 1), ("F", 0), ("A", 2), ("F", 1), ("A", 3), ("B", 0), ("F", 2), ("B", 1), ("A", 4), ("F", 3), ("A", 5),
    ("B", 2), ("C", 0), ("F", 4), ("C", 1), ("A", 6), ("A", 7), ("F", 5), ("B", 3), ("G", 0), ("C", 2), ("B", 4), ("G", 1),
    ("F", 6), ("C", 3), ("F", 7), ("D", 0), ("B", 5), ("G", 2), ("C", 4), ("D", 1), ("B", 6), ("G", 3), ("E", 0), ("C", 5),
    ("D", 2), ("B", 7), ("G", 4), ("E", 1), ("D", 3), ("C", 6), ("G", 5), ("E", 2), ("D", 4), ("C", 7), ("B", 8), ("E", 3),
    ("G", 6), ("D", 5), ("G", 7), ("E", 4), ("C", 8), ("D", 6), ("D", 7), ("E", 5), ("G", 8), ("E", 6), ("E", 7), ("D", 8),
    ("E", 8),
)


def kernel(
    tok, routes, gates, wg, wu, wd, out,
    x_all, w_gu, w_d, meta, gu_own, gu_send, gu_recv, part, xr, ys, yr, zs, zr, fo, flat,
    w_loc, w_send, w_recv, zg_send, zg_recv, mg_send, mg_recv, bg_send, bg_recv, xg_send, xg_recv,
    xf_send, xf_recv, yg_send, yg_recv,
    p_send, p_recv, xr_send, xr_recv, xc_send, xc_recv, yr_send, yr_recv, zr_send, zr_recv, ag_send, ag_recv,
):
    dp = lax.axis_index("dp")
    ex = lax.axis_index("expert")
    pr = lax.axis_index("pair")
    yh, x = dp // NX, lax.rem(dp, NX)
    z, core = ex // NCORE, lax.rem(ex, NCORE)

    def at_z(off):
        return {"expert": lax.rem(z + (off + NZ), NZ) * NCORE + core}

    def at_x(d):
        return {"dp": yh * NX + lax.rem(x + d, NX)}

    x1, x2, x3 = (lax.rem(x + d, NX) for d in (1, 2, 3))

    def at_y(d):
        return {"dp": lax.rem(yh + d, NY) * NX + x}

    def at_dp(d):
        return {"dp": lax.rem(dp + d, NX * NY)}

    sibling = {"expert": z * NCORE + (1 - core)}
    partner = {"pair": 1 - pr}

    def remote(src, dst, send, recv, where):
        return pltpu.make_async_remote_copy(
            src_ref=src, dst_ref=dst, send_sem=send, recv_sem=recv,
            device_id=where, device_id_type=MESH,
        )

    barrier = pltpu.get_barrier_semaphore()
    for k in range(NZ - 1):
        pl.semaphore_signal(barrier, inc=1, device_id=at_z(OFFSETS[k]), device_id_type=MESH)
    for d in range(1, NX * NY):
        pl.semaphore_signal(barrier, inc=1, device_id=at_dp(d), device_id_type=MESH)
    pl.semaphore_signal(barrier, inc=1, device_id=sibling, device_id_type=MESH)
    pl.semaphore_signal(barrier, inc=1, device_id=partner, device_id_type=MESH)

    wcol = pl.multiple_of(core * FFS, FFS)
    wcol_up = pl.multiple_of((NCORE + core) * FFS, FFS)
    w_dsts = (
        (wg.at[0], w_gu.at[:, pl.ds(wcol, FFS)]),
        (wu.at[0], w_gu.at[:, pl.ds(wcol_up, FFS)]),
        (wd.at[0], w_d.at[pl.ds(wcol, FFS)]),
    )
    local = [pltpu.make_async_copy(s, d, w_loc.at[i]) for i, (s, d) in enumerate(w_dsts)]
    own = slice(OWN * BLOCK, NZ * BLOCK)
    mine_in = pltpu.make_async_copy(tok, x_all.at[own], w_loc.at[3])
    mine_in.start()
    for cp in local:
        cp.start()

    flat[...] = jnp.zeros((2 * TOPK, 128), jnp.float32)
    flat[0:TOPK, 0:BLOCK] = routes[...].astype(jnp.float32)
    flat[TOPK:, 0:BLOCK] = gates[...]
    table = jnp.transpose(flat[...])[0:BLOCK]
    lane = lax.broadcasted_iota(jnp.int32, (BLOCK, 128), 1).astype(jnp.float32)
    first = jnp.zeros((BLOCK, 128), jnp.float32)
    second = jnp.zeros((BLOCK, 128), jnp.float32)
    for k in range(TOPK):
        r = table[:, k : k + 1]
        g = table[:, TOPK + k : TOPK + k + 1]
        first = first + jnp.where(lane == r, g, 0.0)
        second = second + jnp.where(lane == r + 32.0, g, 0.0)
    low = second - second.astype(jnp.bfloat16).astype(jnp.float32)
    meta[own, :] = jnp.where(lane < 32, first, low).astype(jnp.bfloat16)
    ys[:, QUART:] = jnp.zeros((TOTAL, NY * SUB - QUART), jnp.bfloat16)

    mine_in.wait()
    pl.semaphore_wait(barrier, NZ - 1 + NX * NY - 1 + 2)

    nb = NB * 128
    na = QUART - nb
    qcol = pl.multiple_of(x * QUART, 128)
    acol = pl.ds(pl.multiple_of(x * na, 128), na)
    bcol = pl.ds(pl.multiple_of(NX * na + yh * nb, 128), nb) if nb else None
    pieces = [(meta, slice(None), mg_send, mg_recv), (x_all, acol, zg_send, zg_recv)]
    if nb:
        pieces.append((x_all, bcol, bg_send, bg_recv))
    sends = []
    zgot = {}

    def hop(src, k):
        step = OFFSETS[k] if src == OWN else (JUMP if OFFSETS[k] > 0 else -JUMP)
        cps = []
        for ref, cols, ssem, rsem in pieces:
            cp = remote(
                ref.at[pl.ds(src * BLOCK, BLOCK), cols], ref.at[pl.ds(k * BLOCK, BLOCK), cols],
                ssem.at[k], rsem.at[k], at_z(step),
            )
            cp.start()
            cps.append(cp)
        zgot[k] = cps
        sends.extend(cps)

    for k in range(2 * JUMP):
        hop(OWN, k)
    weights = [
        remote(s, d, w_send.at[i], w_recv.at[i], sibling) for i, (s, d) in enumerate(w_dsts)
    ]
    for cp in weights:
        cp.start()
    sends += weights

    gathered = {ALONE: []}
    loaded = []
    halves = {}
    paired = {}
    xred = {}
    xcom = {}
    yred = {}
    zred = {}

    def span(j):
        return pl.ds(STARTS[j] * BLOCK, (STARTS[j + 1] - STARTS[j]) * BLOCK)

    def split(j):
        low, count = STARTS[j] * BLOCK, (STARTS[j + 1] - STARTS[j]) * BLOCK // 2
        return pl.ds(low, count), pl.ds(low + count, count)

    def stage_a(j):
        for k in range(STARTS[j], STARTS[j + 1]):
            for cp in zgot[k]:
                cp.wait_recv()
            if k + 2 * JUMP < OWN:
                hop(k, k + 2 * JUMP)
        rows = span(j)
        where = x_all.at[rows, acol]
        cps = [
            remote(where, where, xg_send.at[j, d - 1], xg_recv.at[j, d - 1], at_x(d))
            for d in (1, 3)
        ]
        halves[j] = cps
        ycps = []
        if nb:
            where = x_all.at[rows, bcol]
            ycps = [
                remote(where, where, yg_send.at[j, d - 1], yg_recv.at[j, d - 1], at_y(d))
                for d in (2, 1, 3)
            ]
        for cp in cps + ycps:
            cp.start()
        gathered[j] = list(ycps)
        sends.extend(cps + ycps)

    def stage_f(j):
        for i, (cp, d) in enumerate(zip(halves[j], (1, 3))):
            cp.wait_recv()
            came = pl.ds(pl.multiple_of(lax.rem(x + (NX - d), NX) * na, 128), na)
            where = x_all.at[split(j)[i], came]
            f = remote(where, where, xf_send.at[j, i], xf_recv.at[j, i], at_x(d))
            f.start()
            gathered[j].append(f)
            sends.append(f)

    def stage_b(j):
        if not loaded:
            loaded.append(j)
            for cp in local:
                cp.wait()
            for cp in weights:
                cp.wait_recv()
        for cp in gathered[j]:
            cp.wait_recv()
        rows = span(j)

        def column(n, carry):
            cols = pl.ds(pl.multiple_of(n * 256, 256), 256)
            v = jnp.dot(x_all[rows, :], w_gu[:, cols], preferred_element_type=jnp.float32)
            gu_own[rows, cols] = v
            gu_send[rows, cols] = v.astype(jnp.bfloat16)
            return carry

        lax.fori_loop(0, 2, column, 0)
        cp = remote(gu_send.at[rows], gu_recv.at[rows], p_send.at[j], p_recv.at[j], partner)
        cp.start()
        paired[j] = cp
        sends.append(cp)

    def stage_c(j):
        paired[j].wait_recv()
        rows = span(j)
        m = meta[rows, :].astype(jnp.float32)
        lanes = lax.broadcasted_iota(jnp.int32, m.shape, 1)
        hidden = []
        for c in range(NCORE):
            e = z * NCORE + c
            mine = (lanes == e) | (lanes == e + 32)
            weight = jnp.sum(jnp.where(mine, m, 0.0), axis=1, keepdims=True)
            gcols = slice(c * FFS, (c + 1) * FFS)
            ucols = slice((NCORE + c) * FFS, (NCORE + c + 1) * FFS)
            g = gu_own[rows, gcols] + gu_recv[rows, gcols].astype(jnp.float32)
            u = gu_own[rows, ucols] + gu_recv[rows, ucols].astype(jnp.float32)
            h = (0.5 * g) * (1.0 + jnp.tanh(0.5 * g)) * u * weight
            hidden.append(h.astype(jnp.bfloat16))
        hidden = jnp.concatenate(hidden, axis=1)
        def quarter(q, carry):
            v = jnp.dot(
                hidden, w_d[:, pl.ds(pl.multiple_of(q * QUART, 128), QUART)],
                preferred_element_type=jnp.float32,
            )
            part[q, rows, :] = v.astype(jnp.bfloat16)
            return carry

        lax.fori_loop(0, NX, quarter, 0)
        low, high = split(j)
        cps = []
        for i, (d, q, half, slot) in enumerate(
            ((1, x2, low, 2), (3, x2, high, 3), (1, x1, high, 0), (3, x3, low, 1))
        ):
            cp = remote(
                part.at[q, half], xr.at[slot, half], xr_send.at[j, i], xr_recv.at[j, i], at_x(d)
            )
            cp.start()
            cps.append(cp)
        xred[j] = cps
        sends.extend(cps)

    def stage_g(j):
        low, high = split(j)
        cps = []
        for i, (d, q, half) in enumerate(((1, x1, low), (3, x3, high))):
            xred[j][i].wait_recv()
            v = part[q, half, :].astype(jnp.float32) + xr[2 + i, half, :].astype(jnp.float32)
            part[q, half, :] = v.astype(jnp.bfloat16)
            cp = remote(
                part.at[q, half], xr.at[i, half], xc_send.at[j, i], xc_recv.at[j, i], at_x(d)
            )
            cp.start()
            cps.append(cp)
        xcom[j] = cps
        sends.extend(cps)

    def stage_d(j):
        for cp in xred[j][2:] + xcom[j]:
            cp.wait_recv()
        rows = span(j)
        total = part[x, rows, :].astype(jnp.float32)
        for d in range(2):
            total = total + xr[d, rows, :].astype(jnp.float32)
        ys[rows, 0:QUART] = total.astype(jnp.bfloat16)
        cps = []
        for d in (2, 1, 3):
            scol = pl.multiple_of(lax.rem(yh + d, NY) * SUB, SUB)
            cp = remote(
                ys.at[rows, pl.ds(scol, SUB)], yr.at[d - 1, rows],
                yr_send.at[j, d - 1], yr_recv.at[j, d - 1], at_y(d),
            )
            cp.start()
            cps.append(cp)
        yred[j] = cps
        sends.extend(cps)

    def stage_e(j):
        for cp in yred[j]:
            cp.wait_recv()
        rows = span(j)
        total = ys[rows, pl.ds(pl.multiple_of(yh * SUB, SUB), SUB)].astype(jnp.float32)
        for d in range(NY - 1):
            total = total + yr[d, rows, :].astype(jnp.float32)
        zs[rows, :] = total.astype(jnp.bfloat16)
        for k in range(STARTS[j], STARTS[j + 1]):
            if k != OWN:
                cp = remote(
                    zs.at[pl.ds(k * BLOCK, BLOCK)], zr.at[k],
                    zr_send.at[k], zr_recv.at[k], at_z(-OFFSETS[k]),
                )
                cp.start()
                zred[k] = cp
                sends.append(cp)

    stages = dict(A=stage_a, F=stage_f, G=stage_g, B=stage_b, C=stage_c, D=stage_d, E=stage_e)
    for name, j in ORDER:
        stages[name](j)

    total = zs[own, :].astype(jnp.float32)
    for k in range(NZ - 1):
        zred[k].wait_recv()
        total = total + zr[k].astype(jnp.float32)
    fo[dp] = total.astype(jnp.bfloat16)
    last = []
    for d in range(1, NX * NY):
        cp = remote(fo.at[dp], fo.at[dp], ag_send.at[d], ag_recv.at[d], at_dp(d))
        cp.start()
        last.append(cp)
    sends += last
    for cp in last:
        cp.wait_recv()
    for b in range(NY):
        for a in range(NX):
            width = min(SUB, QUART - b * SUB)
            start = a * QUART + b * SUB
            out[:, start : start + width] = fo[b * NX + a, :, 0:width]
    for cp in sends:
        cp.wait_send()


def per_device(tokens, routes, gates, w_gate, w_up, w_down):
    total = TOTAL
    bf, f32 = jnp.bfloat16, jnp.float32
    dma = pltpu.SemaphoreType.DMA
    vm = pl.BlockSpec(memory_space=pltpu.VMEM)
    hbm = pl.BlockSpec(memory_space=pl.ANY)
    return pl.pallas_call(
        kernel,
        out_shape=jax.ShapeDtypeStruct((BLOCK, HALF), bf),
        in_specs=[hbm, vm, vm, hbm, hbm, hbm],
        out_specs=vm,
        scratch_shapes=[
            pltpu.VMEM((total, HALF), bf),
            pltpu.VMEM((HALF, 2 * NCORE * FFS), bf),
            pltpu.VMEM((NCORE * FFS, HALF), bf),
            pltpu.VMEM((total, 128), bf),
            pltpu.VMEM((total, 2 * NCORE * FFS), f32),
            pltpu.VMEM((total, 2 * NCORE * FFS), bf),
            pltpu.VMEM((total, 2 * NCORE * FFS), bf),
            pltpu.VMEM((NX, total, QUART), bf),
            pltpu.VMEM((NX, total, QUART), bf),
            pltpu.VMEM((total, NY * SUB), bf),
            pltpu.VMEM((NY - 1, total, SUB), bf),
            pltpu.VMEM((total, SUB), bf),
            pltpu.VMEM((NZ, BLOCK, SUB), bf),
            pltpu.VMEM((NX * NY, BLOCK, SUB), bf),
            pltpu.VMEM((2 * TOPK, 128), f32),
            dma((4,)), dma((3,)), dma((3,)),
            dma((NZ,)), dma((NZ,)), dma((NZ,)), dma((NZ,)),
            dma((NZ,)), dma((NZ,)),
            dma((CHUNKS, NX - 1)), dma((CHUNKS, NX - 1)),
            dma((CHUNKS, 2)), dma((CHUNKS, 2)),
            dma((CHUNKS, NY - 1)), dma((CHUNKS, NY - 1)),
            dma((CHUNKS,)), dma((CHUNKS,)),
            dma((CHUNKS, 4)), dma((CHUNKS, 4)),
            dma((CHUNKS, 2)), dma((CHUNKS, 2)),
            dma((CHUNKS, NY - 1)), dma((CHUNKS, NY - 1)),
            dma((NZ,)), dma((NZ,)),
            dma((NX * NY,)), dma((NX * NY,)),
        ],
        compiler_params=pltpu.CompilerParams(
            collective_id=0, has_side_effects=True, vmem_limit_bytes=60 << 20
        ),
        cost_estimate=pl.CostEstimate(flops=2 * 3 * 512 * 3584 * 256, bytes_accessed=4 << 20, transcendentals=512 * 256),
    )(tokens, routes.T, gates.T, w_gate, w_up, w_down)


def solution(mesh):
    placed = (
        P("expert", "pair"),
        P("expert", None),
        P("expert", None),
        P("expert", "pair", "dp"),
        P("expert", "pair", "dp"),
        P("expert", "dp", "pair"),
    )
    return jax.shard_map(
        per_device, mesh=mesh, in_specs=placed, out_specs=P("expert", "pair"), check_vma=False
    )
```

```python
import jax
import jax.numpy as jnp
from jax import lax
from jax.experimental import pallas as pl
from jax.experimental.pallas import tpu as pltpu
from jax.sharding import PartitionSpec as P

MESH = pl.DeviceIdType.MESH
NX = 4
NY = 4
NZ = 16
NCORE = 2
BLOCK = 32
HALF = 3584
QUART = 896
SUB = 256
FFS = 128
STARTS = (0, 2, 4, 6, 8, 10, 12, 14, 15, 16)
CHUNKS = 9
ALONE = CHUNKS - 1
NB = 2
TOTAL = 512
OFFSETS = (1, -1, 2, -2, 3, -3, 4, -4, 5, -5, 6, -6, 7, -7, 8, 0)
OWN = NZ - 1
JUMP = 2
TOPK = 8
ORDER = (
    ("A", 0), ("A", 1), ("F", 0), ("A", 2), ("F", 1), ("A", 3), ("B", 0), ("F", 2), ("B", 1), ("A", 4), ("F", 3), ("A", 5),
    ("B", 2), ("C", 0), ("F", 4), ("C", 1), ("A", 6), ("A", 7), ("F", 5), ("B", 3), ("G", 0), ("C", 2), ("B", 4), ("G", 1),
    ("F", 6), ("C", 3), ("F", 7), ("D", 0), ("B", 5), ("G", 2), ("C", 4), ("D", 1), ("B", 6), ("G", 3), ("E", 0), ("C", 5),
    ("D", 2), ("B", 7), ("G", 4), ("E", 1), ("D", 3), ("C", 6), ("G", 5), ("E", 2), ("D", 4), ("C", 7), ("B", 8), ("E", 3),
    ("G", 6), ("D", 5), ("G", 7), ("E", 4), ("C", 8), ("D", 6), ("D", 7), ("E", 5), ("G", 8), ("E", 6), ("E", 7), ("D", 8),
    ("E", 8),
)


def kernel(
    tok, routes, gates, wg, wu, wd, out,
    x_all, w_gu, w_d, meta, gu_own, gu_send, gu_recv, part, xr, ys, yr, zs, zr, fo, flat,
    w_loc, w_send, w_recv, zg_send, zg_recv, mg_send, mg_recv, bg_send, bg_recv, xg_send, xg_recv,
    xf_send, xf_recv, yg_send, yg_recv,
    p_send, p_recv, xr_send, xr_recv, xc_send, xc_recv, yr_send, yr_recv, zr_send, zr_recv, ag_send, ag_recv,
):
    dp = lax.axis_index("dp")
    ex = lax.axis_index("expert")
    pr = lax.axis_index("pair")
    yh, x = dp // NX, lax.rem(dp, NX)
    z, core = ex // NCORE, lax.rem(ex, NCORE)

    def at_z(off):
        return {"expert": lax.rem(z + (off + NZ), NZ) * NCORE + core}

    def at_x(d):
        return {"dp": yh * NX + lax.rem(x + d, NX)}

    x1, x2, x3 = (lax.rem(x + d, NX) for d in (1, 2, 3))

    def at_y(d):
        return {"dp": lax.rem(yh + d, NY) * NX + x}

    def at_dp(d):
        return {"dp": lax.rem(dp + d, NX * NY)}

    sibling = {"expert": z * NCORE + (1 - core)}
    partner = {"pair": 1 - pr}

    def remote(src, dst, send, recv, where):
        return pltpu.make_async_remote_copy(
            src_ref=src, dst_ref=dst, send_sem=send, recv_sem=recv,
            device_id=where, device_id_type=MESH,
        )

    barrier = pltpu.get_barrier_semaphore()
    near = [at_z(off) for off in OFFSETS[: 2 * JUMP]]
    near += [at_x(d) for d in range(1, NX)] + [at_y(d) for d in range(1, NY)]
    for where in near:
        pl.semaphore_signal(barrier, inc=1, device_id=where, device_id_type=MESH)
    pl.semaphore_signal(barrier, inc=1, device_id=sibling, device_id_type=MESH)
    pl.semaphore_signal(barrier, inc=1, device_id=partner, device_id_type=MESH)

    wcol = pl.multiple_of(core * FFS, FFS)
    wcol_up = pl.multiple_of((NCORE + core) * FFS, FFS)
    w_dsts = (
        (wg.at[0], w_gu.at[:, pl.ds(wcol, FFS)]),
        (wu.at[0], w_gu.at[:, pl.ds(wcol_up, FFS)]),
        (wd.at[0], w_d.at[pl.ds(wcol, FFS)]),
    )
    local = [pltpu.make_async_copy(s, d, w_loc.at[i]) for i, (s, d) in enumerate(w_dsts)]
    own = slice(OWN * BLOCK, NZ * BLOCK)
    mine_in = pltpu.make_async_copy(tok, x_all.at[own], w_loc.at[3])
    mine_in.start()
    for cp in local:
        cp.start()

    flat[...] = jnp.zeros((2 * TOPK, 128), jnp.float32)
    flat[0:TOPK, 0:BLOCK] = routes[...].astype(jnp.float32)
    flat[TOPK:, 0:BLOCK] = gates[...]
    table = jnp.transpose(flat[...])[0:BLOCK]
    lane = lax.broadcasted_iota(jnp.int32, (BLOCK, 128), 1).astype(jnp.float32)
    first = jnp.zeros((BLOCK, 128), jnp.float32)
    second = jnp.zeros((BLOCK, 128), jnp.float32)
    for k in range(TOPK):
        r = table[:, k : k + 1]
        g = table[:, TOPK + k : TOPK + k + 1]
        first = first + jnp.where(lane == r, g, 0.0)
        second = second + jnp.where(lane == r + 32.0, g, 0.0)
    low = second - second.astype(jnp.bfloat16).astype(jnp.float32)
    meta[own, :] = jnp.where(lane < 32, first, low).astype(jnp.bfloat16)
    ys[:, QUART:] = jnp.zeros((TOTAL, NY * SUB - QUART), jnp.bfloat16)

    mine_in.wait()
    pl.semaphore_wait(barrier, len(near) + 2)

    nb = NB * 128
    na = QUART - nb
    qcol = pl.multiple_of(x * QUART, 128)
    acol = pl.ds(pl.multiple_of(x * na, 128), na)
    bcol = pl.ds(pl.multiple_of(NX * na + yh * nb, 128), nb) if nb else None
    pieces = [(meta, slice(None), mg_send, mg_recv), (x_all, acol, zg_send, zg_recv)]
    if nb:
        pieces.append((x_all, bcol, bg_send, bg_recv))
    sends = []
    zgot = {}

    def hop(src, k):
        step = OFFSETS[k] if src == OWN else (JUMP if OFFSETS[k] > 0 else -JUMP)
        cps = []
        for ref, cols, ssem, rsem in pieces:
            cp = remote(
                ref.at[pl.ds(src * BLOCK, BLOCK), cols], ref.at[pl.ds(k * BLOCK, BLOCK), cols],
                ssem.at[k], rsem.at[k], at_z(step),
            )
            cp.start()
            cps.append(cp)
        zgot[k] = cps
        sends.extend(cps)

    for k in range(2 * JUMP):
        hop(OWN, k)
    weights = [
        remote(s, d, w_send.at[i], w_recv.at[i], sibling) for i, (s, d) in enumerate(w_dsts)
    ]
    for cp in weights:
        cp.start()
    sends += weights

    gathered = {ALONE: []}
    loaded = []
    halves = {}
    paired = {}
    xred = {}
    xcom = {}
    yred = {}
    zred = {}

    def span(j):
        return pl.ds(STARTS[j] * BLOCK, (STARTS[j + 1] - STARTS[j]) * BLOCK)

    def split(j):
        low, count = STARTS[j] * BLOCK, (STARTS[j + 1] - STARTS[j]) * BLOCK // 2
        return pl.ds(low, count), pl.ds(low + count, count)

    def stage_a(j):
        for k in range(STARTS[j], STARTS[j + 1]):
            for cp in zgot[k]:
                cp.wait_recv()
            if k + 2 * JUMP < OWN:
                hop(k, k + 2 * JUMP)
        rows = span(j)
        where = x_all.at[rows, acol]
        cps = [
            remote(where, where, xg_send.at[j, d - 1], xg_recv.at[j, d - 1], at_x(d))
            for d in (1, 3)
        ]
        halves[j] = cps
        ycps = []
        if nb:
            where = x_all.at[rows, bcol]
            ycps = [
                remote(where, where, yg_send.at[j, d - 1], yg_recv.at[j, d - 1], at_y(d))
                for d in (2, 1, 3)
            ]
        for cp in cps + ycps:
            cp.start()
        gathered[j] = list(ycps)
        sends.extend(cps + ycps)

    def stage_f(j):
        for i, (cp, d) in enumerate(zip(halves[j], (1, 3))):
            cp.wait_recv()
            came = pl.ds(pl.multiple_of(lax.rem(x + (NX - d), NX) * na, 128), na)
            where = x_all.at[split(j)[i], came]
            f = remote(where, where, xf_send.at[j, i], xf_recv.at[j, i], at_x(d))
            f.start()
            gathered[j].append(f)
            sends.append(f)

    def stage_b(j):
        if not loaded:
            loaded.append(j)
            for cp in local:
                cp.wait()
            for cp in weights:
                cp.wait_recv()
        for cp in gathered[j]:
            cp.wait_recv()
        rows = span(j)

        def column(n, carry):
            cols = pl.ds(pl.multiple_of(n * 256, 256), 256)
            v = jnp.dot(x_all[rows, :], w_gu[:, cols], preferred_element_type=jnp.float32)
            gu_own[rows, cols] = v
            gu_send[rows, cols] = v.astype(jnp.bfloat16)
            return carry

        lax.fori_loop(0, 2, column, 0)
        cp = remote(gu_send.at[rows], gu_recv.at[rows], p_send.at[j], p_recv.at[j], partner)
        cp.start()
        paired[j] = cp
        sends.append(cp)

    def stage_c(j):
        paired[j].wait_recv()
        rows = span(j)
        m = meta[rows, :].astype(jnp.float32)
        lanes = lax.broadcasted_iota(jnp.int32, m.shape, 1)
        hidden = []
        for c in range(NCORE):
            e = z * NCORE + c
            mine = (lanes == e) | (lanes == e + 32)
            weight = jnp.sum(jnp.where(mine, m, 0.0), axis=1, keepdims=True)
            gcols = slice(c * FFS, (c + 1) * FFS)
            ucols = slice((NCORE + c) * FFS, (NCORE + c + 1) * FFS)
            g = gu_own[rows, gcols] + gu_recv[rows, gcols].astype(jnp.float32)
            u = gu_own[rows, ucols] + gu_recv[rows, ucols].astype(jnp.float32)
            h = (0.5 * g) * (1.0 + jnp.tanh(0.5 * g)) * u * weight
            hidden.append(h.astype(jnp.bfloat16))
        hidden = jnp.concatenate(hidden, axis=1)
        def quarter(q, carry):
            v = jnp.dot(
                hidden, w_d[:, pl.ds(pl.multiple_of(q * QUART, 128), QUART)],
                preferred_element_type=jnp.float32,
            )
            part[q, rows, :] = v.astype(jnp.bfloat16)
            return carry

        lax.fori_loop(0, NX, quarter, 0)
        low, high = split(j)
        cps = []
        for i, (d, q, half, slot) in enumerate(
            ((1, x2, low, 2), (3, x2, high, 3), (1, x1, high, 0), (3, x3, low, 1))
        ):
            cp = remote(
                part.at[q, half], xr.at[slot, half], xr_send.at[j, i], xr_recv.at[j, i], at_x(d)
            )
            cp.start()
            cps.append(cp)
        xred[j] = cps
        sends.extend(cps)

    def stage_g(j):
        low, high = split(j)
        cps = []
        for i, (d, q, half) in enumerate(((1, x1, low), (3, x3, high))):
            xred[j][i].wait_recv()
            v = part[q, half, :].astype(jnp.float32) + xr[2 + i, half, :].astype(jnp.float32)
            part[q, half, :] = v.astype(jnp.bfloat16)
            cp = remote(
                part.at[q, half], xr.at[i, half], xc_send.at[j, i], xc_recv.at[j, i], at_x(d)
            )
            cp.start()
            cps.append(cp)
        xcom[j] = cps
        sends.extend(cps)

    def stage_d(j):
        for cp in xred[j][2:] + xcom[j]:
            cp.wait_recv()
        rows = span(j)
        total = part[x, rows, :].astype(jnp.float32)
        for d in range(2):
            total = total + xr[d, rows, :].astype(jnp.float32)
        ys[rows, 0:QUART] = total.astype(jnp.bfloat16)
        cps = []
        for d in (2, 1, 3):
            scol = pl.multiple_of(lax.rem(yh + d, NY) * SUB, SUB)
            cp = remote(
                ys.at[rows, pl.ds(scol, SUB)], yr.at[d - 1, rows],
                yr_send.at[j, d - 1], yr_recv.at[j, d - 1], at_y(d),
            )
            cp.start()
            cps.append(cp)
        yred[j] = cps
        sends.extend(cps)

    def stage_e(j):
        for cp in yred[j]:
            cp.wait_recv()
        rows = span(j)
        total = ys[rows, pl.ds(pl.multiple_of(yh * SUB, SUB), SUB)].astype(jnp.float32)
        for d in range(NY - 1):
            total = total + yr[d, rows, :].astype(jnp.float32)
        zs[rows, :] = total.astype(jnp.bfloat16)
        for k in range(STARTS[j], STARTS[j + 1]):
            if k != OWN:
                cp = remote(
                    zs.at[pl.ds(k * BLOCK, BLOCK)], zr.at[k],
                    zr_send.at[k], zr_recv.at[k], at_z(-OFFSETS[k]),
                )
                cp.start()
                zred[k] = cp
                sends.append(cp)

    stages = dict(A=stage_a, F=stage_f, G=stage_g, B=stage_b, C=stage_c, D=stage_d, E=stage_e)
    for name, j in ORDER:
        stages[name](j)

    total = zs[own, :].astype(jnp.float32)
    for k in range(NZ - 1):
        zred[k].wait_recv()
        total = total + zr[k].astype(jnp.float32)
    fo[dp] = total.astype(jnp.bfloat16)
    last = []
    for d in range(1, NX * NY):
        cp = remote(fo.at[dp], fo.at[dp], ag_send.at[d], ag_recv.at[d], at_dp(d))
        cp.start()
        last.append(cp)
    sends += last
    for cp in last:
        cp.wait_recv()
    for b in range(NY):
        for a in range(NX):
            width = min(SUB, QUART - b * SUB)
            start = a * QUART + b * SUB
            out[:, start : start + width] = fo[b * NX + a, :, 0:width]
    for cp in sends:
        cp.wait_send()


def per_device(tokens, routes, gates, w_gate, w_up, w_down):
    total = TOTAL
    bf, f32 = jnp.bfloat16, jnp.float32
    dma = pltpu.SemaphoreType.DMA
    vm = pl.BlockSpec(memory_space=pltpu.VMEM)
    hbm = pl.BlockSpec(memory_space=pl.ANY)
    return pl.pallas_call(
        kernel,
        out_shape=jax.ShapeDtypeStruct((BLOCK, HALF), bf),
        in_specs=[hbm, vm, vm, hbm, hbm, hbm],
        out_specs=vm,
        scratch_shapes=[
            pltpu.VMEM((total, HALF), bf),
            pltpu.VMEM((HALF, 2 * NCORE * FFS), bf),
            pltpu.VMEM((NCORE * FFS, HALF), bf),
            pltpu.VMEM((total, 128), bf),
            pltpu.VMEM((total, 2 * NCORE * FFS), f32),
            pltpu.VMEM((total, 2 * NCORE * FFS), bf),
            pltpu.VMEM((total, 2 * NCORE * FFS), bf),
            pltpu.VMEM((NX, total, QUART), bf),
            pltpu.VMEM((NX, total, QUART), bf),
            pltpu.VMEM((total, NY * SUB), bf),
            pltpu.VMEM((NY - 1, total, SUB), bf),
            pltpu.VMEM((total, SUB), bf),
            pltpu.VMEM((NZ, BLOCK, SUB), bf),
            pltpu.VMEM((NX * NY, BLOCK, SUB), bf),
            pltpu.VMEM((2 * TOPK, 128), f32),
            dma((4,)), dma((3,)), dma((3,)),
            dma((NZ,)), dma((NZ,)), dma((NZ,)), dma((NZ,)),
            dma((NZ,)), dma((NZ,)),
            dma((CHUNKS, NX - 1)), dma((CHUNKS, NX - 1)),
            dma((CHUNKS, 2)), dma((CHUNKS, 2)),
            dma((CHUNKS, NY - 1)), dma((CHUNKS, NY - 1)),
            dma((CHUNKS,)), dma((CHUNKS,)),
            dma((CHUNKS, 4)), dma((CHUNKS, 4)),
            dma((CHUNKS, 2)), dma((CHUNKS, 2)),
            dma((CHUNKS, NY - 1)), dma((CHUNKS, NY - 1)),
            dma((NZ,)), dma((NZ,)),
            dma((NX * NY,)), dma((NX * NY,)),
        ],
        compiler_params=pltpu.CompilerParams(
            collective_id=0, has_side_effects=True, vmem_limit_bytes=60 << 20
        ),
        cost_estimate=pl.CostEstimate(flops=2 * 3 * 512 * 3584 * 256, bytes_accessed=4 << 20, transcendentals=512 * 256),
    )(tokens, routes.T, gates.T, w_gate, w_up, w_down)


def solution(mesh):
    placed = (
        P("expert", "pair"),
        P("expert", None),
        P("expert", None),
        P("expert", "pair", "dp"),
        P("expert", "pair", "dp"),
        P("expert", "dp", "pair"),
    )
    return jax.shard_map(
        per_device, mesh=mesh, in_specs=placed, out_specs=P("expert", "pair"), check_vma=False
    )
```
